32 devices in a mesh: row: 4 (over y, x), col: 8 (over z, core).
Axes of the slice: x: 2, y: 2, z: 4, core: 2. Of those that a mesh axis runs over, the one named last changes fastest.
Arguments:
- panel: bfloat16 [4, 4, 512, 512], P(None, 'row', 'col'), may hold values from -1.1953125 to 1.1953125
- inverse_factor: bfloat16 [512, 512], replicated
- slot_rows: int32 [4, 8, 2], P('row', 'col'), may hold values from 0 to 15, as said below
- slot_cols: int32 [4, 8, 2], P('row', 'col'), may hold values from 0 to 15, as said below
- live_count: int32 [4, 8], P('row', 'col'), may hold values from 0 to 2
Outputs:
- contrib: bfloat16 [4, 8, 2, 512, 512], P('row', 'col')
The draws below stay inside these ranges and needn't reach their ends.
Inputs may be any that keep to these rules, and one draw needn't show every extreme that they name: slot_rows[r, c, s] is congruent to r modulo 4; for s < live_count[r, c] the slots of one position name distinct blocks with slot_rows >= slot_cols; the other slots are ignored. slot_cols[r, c, s] is congruent to c modulo 8.
All inputs are finite; a program needn't handle non-finite values.
Results may differ from the reference program's by a relative error of at most 0.0054.
Values may be sent and summed in bfloat16 or wider, within the bound.
A program may use at most 64 MiB of HBM per device.

```python
import jax
import jax.numpy as jnp
from jax import lax

B = 512
PR = 4
SLOTS = 2
N_ROW = 4
N_COL = 8


def slot_plan(key):
    col_ratio = N_COL // N_ROW
    per_row = PR // col_ratio
    count = PR * per_row
    candidate = jnp.arange(count, dtype=jnp.int32)
    cand_a = candidate // per_row
    cand_b = candidate % per_row
    row_index = jnp.arange(N_ROW, dtype=jnp.int32)[:, None, None]
    col_index = jnp.arange(N_COL, dtype=jnp.int32)[None, :, None]
    valid = row_index + N_ROW * cand_a >= col_index + N_COL * cand_b
    scores = jax.random.randint(jax.random.fold_in(key, 11), (N_ROW, N_COL, count), 0, 4096) * count + candidate
    scores = scores + jnp.where(valid, 0, 1 << 24)
    first_corner = (row_index == 0) & (col_index == 0) & (candidate[None, None, :] == 0)
    last_corner = (row_index == N_ROW - 1) & (col_index == N_COL - 1) & (candidate[None, None, :] == count - 1)
    scores = scores - jnp.where(first_corner | last_corner, 1 << 25, 0)
    order = jnp.argsort(scores, axis=-1)[..., :SLOTS].astype(jnp.int32)
    chosen_valid = jnp.take_along_axis(valid, order, axis=-1)
    pick_a = jnp.where(chosen_valid, order // per_row, 0)
    pick_b = jnp.where(chosen_valid, order % per_row, 0)
    rows_out = (row_index + N_ROW * pick_a).astype(jnp.int32)
    cols_out = (col_index + N_COL * pick_b).astype(jnp.int32)
    valid_count = jnp.sum(valid.astype(jnp.int32), axis=-1)
    wanted = jax.random.randint(jax.random.fold_in(key, 12), (N_ROW, N_COL), 1, SLOTS + 1)
    full_row = jax.random.randint(jax.random.fold_in(key, 13), (), 0, N_ROW)
    full_col = jax.random.randint(jax.random.fold_in(key, 14), (), 0, full_row + 1)
    forced = (jnp.arange(N_ROW)[:, None] == full_row) & (jnp.arange(N_COL)[None, :] == full_col)
    wanted = jnp.where(forced, SLOTS, wanted)
    live = jnp.minimum(valid_count, wanted).astype(jnp.int32)
    return (rows_out, cols_out, live)


def draw_slot_rows(key, part):
    return slot_plan(key)[0]


def draw_slot_cols(key, part):
    return slot_plan(key)[1]


def draw_live_count(key, part):
    return slot_plan(key)[2]


def draw_inverse_factor(key, part):
    diagonal = jnp.exp(jax.random.uniform(jax.random.fold_in(key, 21), (B,), minval=-0.7, maxval=0.7))
    upper_part = 0.035 * jax.random.normal(jax.random.fold_in(key, 22), (B, B))
    matrix = jnp.triu(upper_part, 1) + jnp.diag(diagonal)
    return matrix.astype(jnp.float32).astype(jnp.bfloat16)


def shard_levels(stream_key, shape, shards, low, high):
    gain, own = 1.0, jax.random.fold_in(stream_key, 6)
    for dim, parts in shards:
        steps = jnp.exp(jax.random.uniform(jax.random.fold_in(own, dim), (parts,), jnp.float32, low / len(shards), high / len(shards)))
        gain = gain * jnp.repeat(steps, shape[dim] // parts).reshape([-1 if axis == dim else 1 for axis in range(len(shape))])
    return gain


def normal_values(rng, shape, deviation, limit, split=(), kind=jnp.bfloat16):
    array = deviation * jax.random.normal(rng, shape, jnp.float32)
    if split:
        array = array * shard_levels(rng, shape, split, -0.22, 0.18)
    return jnp.clip(array, -limit, limit).astype(kind)


def setup_inputs(seed: int = 0) -> dict:
    key_list = jax.random.split(jax.random.key(seed), 6)
    panel = normal_values(key_list[0], (PR, N_ROW, B, B), 0.2, 1.1953125, ((1, 4), (2, 8)))
    inverse_factor = draw_inverse_factor(jax.random.fold_in(key_list[5], 71), 0)
    slot_rows = draw_slot_rows(jax.random.fold_in(key_list[5], 71), 0)
    slot_cols = draw_slot_cols(jax.random.fold_in(key_list[5], 71), 0)
    live_count = draw_live_count(jax.random.fold_in(key_list[5], 71), 0)
    return {"panel": panel, "inverse_factor": inverse_factor, "slot_rows": slot_rows, "slot_cols": slot_cols, "live_count": live_count}


def reference(panel, inverse_factor, slot_rows, slot_cols, live_count):
    factor = jnp.dot(panel.reshape(-1, B), inverse_factor, preferred_element_type=jnp.float32)
    factor = factor.astype(jnp.bfloat16).reshape(PR * N_ROW, B, B)
    slot_index = jnp.arange(SLOTS, dtype=jnp.int32)
    live_mask = (slot_index[None, None, :] < live_count[:, :, None]).reshape(-1)
    flat_rows = slot_rows.reshape(-1).astype(jnp.int32)
    flat_cols = slot_cols.reshape(-1).astype(jnp.int32)

    def slot_tile(item):
        block_row, block_col, flag = item
        left_tile = lax.dynamic_index_in_dim(factor, block_row, 0, keepdims=False)
        right_tile = lax.dynamic_index_in_dim(factor, block_col, 0, keepdims=False)
        product = jnp.dot(left_tile, right_tile.T, preferred_element_type=jnp.float32)
        return jnp.where(flag, -product, jnp.zeros_like(product)).astype(jnp.bfloat16)

    tiles = lax.map(slot_tile, (flat_rows, flat_cols, live_mask))
    return tiles.reshape(N_ROW, N_COL, SLOTS, B, B)
```

```python
import functools
import math

import jax
import jax.numpy as jnp
from jax import lax
from jax.experimental import pallas as pl
from jax.experimental.pallas import tpu as pltpu
from jax.sharding import PartitionSpec as P

MESH = pl.DeviceIdType.MESH


def row_sides(grid_rows):
    width = math.isqrt(grid_rows)
    while grid_rows % width:
        width -= 1
    return grid_rows // width, width


def kernel(
    grid_rows,
    grid_cols,
    panel_ref,
    inverse_ref,
    slot_rows_ref,
    slot_cols_ref,
    live_ref,
    out_ref,
    panel_buf,
    inverse_buf,
    rows,
    cols,
    result,
    load_sem,
    store_sem,
    local_sem,
    up_send,
    up_recv,
    down_send,
    down_recv,
    sib_send,
    sib_recv,
    y_send,
    x_send,
    col_recv,
):
    depth = grid_cols // 2
    height, width = row_sides(grid_rows)
    column_count, col_ratio, tile, _ = rows.shape
    part = tile // grid_cols
    slot_total = result.shape[0]

    r = lax.axis_index("row")
    c = lax.axis_index("col")
    y, x = r // width, lax.rem(r, width)
    z, core = c // 2, lax.rem(c, 2)
    other = 1 - core
    own_group = c // grid_rows
    source = lax.rem(c, grid_rows)
    source_y, source_x = source // width, lax.rem(source, width)
    is_source = r == source
    on_source_x = x == source_x
    relays = jnp.logical_and(on_source_x, y != source_y)

    load_panel = pltpu.make_async_copy(panel_ref, panel_buf, load_sem.at[0])
    load_inverse = pltpu.make_async_copy(inverse_ref, inverse_buf, load_sem.at[1])
    load_panel.start()
    load_inverse.start()

    barrier = pltpu.get_barrier_semaphore()

    def greet(row, col):
        pl.semaphore_signal(barrier, inc=1, device_id=(row, col), device_id_type=MESH)

    greet(r, 2 * z + other)
    for step in range(1, width):
        greet(y * width + lax.rem(x + step, width), c)
    for step in range(1, height):
        greet(lax.rem(y + step, height) * width + x, c)
    can_up, can_down = z + 1 < depth, z > 0

    @pl.when(can_up)
    def _():
        greet(r, c + 2)

    @pl.when(can_down)
    def _():
        greet(r, c - 2)

    def band(piece):
        return pl.ds(pl.multiple_of(piece * part, part), part)

    load_panel.wait()
    load_inverse.wait()
    solved = jnp.dot(
        panel_buf[...].reshape(-1, tile), inverse_buf[...], preferred_element_type=jnp.float32
    )
    solved = solved.astype(jnp.bfloat16).reshape(column_count, col_ratio, part, tile)
    rows[:, :, band(c), :] = solved

    line_peers = can_up.astype(jnp.int32) + can_down.astype(jnp.int32)
    pl.semaphore_wait(barrier, 1 + (width - 1) + (height - 1) + line_peers)

    def up(dist, group):
        chunk = rows.at[:, group, band(c - 2 * dist)]
        return pltpu.make_async_remote_copy(
            chunk, chunk, up_send.at[dist, group], up_recv.at[dist, group], (r, c + 2), MESH
        )

    def up_arrival(dist, group):
        chunk = rows.at[:, group, band(c - 2 * dist)]
        return pltpu.make_async_remote_copy(
            chunk, chunk, up_send.at[dist, group], up_recv.at[dist - 1, group], (r, c - 2), MESH
        )

    def down(dist, group):
        chunk = rows.at[:, group, band(c + 2 * dist)]
        return pltpu.make_async_remote_copy(
            chunk, chunk, down_send.at[dist, group], down_recv.at[dist, group], (r, c - 2), MESH
        )

    def down_arrival(dist, group):
        chunk = rows.at[:, group, band(c + 2 * dist)]
        return pltpu.make_async_remote_copy(
            chunk, chunk, down_send.at[dist, group], down_recv.at[dist - 1, group], (r, c + 2), MESH
        )

    def sibling(level, group, sender):
        chunk = rows.at[:, group, band(2 * level + sender)]
        return pltpu.make_async_remote_copy(
            chunk,
            chunk,
            sib_send.at[level, group],
            sib_recv.at[level, group],
            (r, 2 * z + other),
            MESH,
        )

    def along_y(piece, step):
        return pltpu.make_async_remote_copy(
            rows.at[:, own_group, band(piece)],
            cols.at[:, band(piece)],
            y_send.at[step - 1, piece],
            col_recv.at[piece],
            (lax.rem(y + step, height) * width + x, c),
            MESH,
        )

    def along_x(piece, step, origin):
        return pltpu.make_async_remote_copy(
            origin,
            cols.at[:, band(piece)],
            x_send.at[step - 1, piece],
            col_recv.at[piece],
            (y * width + lax.rem(x + step, width), c),
            MESH,
        )

    def keep(piece):
        return pltpu.make_async_copy(
            rows.at[:, own_group, band(piece)], cols.at[:, band(piece)], local_sem.at[piece]
        )

    def column_send(piece):
        for step in range(1, height):
            along_y(piece, step).start()
        for step in range(1, width):
            along_x(piece, step, rows.at[:, own_group, band(piece)]).start()
        keep(piece).start()

    def column_arrival(piece):
        return along_x(piece, 1, cols.at[:, band(piece)])

    def column_relay(piece):
        column_arrival(piece).wait_recv()
        for step in range(1, width):
            along_x(piece, step, cols.at[:, band(piece)]).start()

    def levels(dist):
        if dist == 0:
            return [(z, None)]
        return [(z - dist, z >= dist), (z + dist, z + dist < depth)]

    def guarded(condition, action):
        if condition is None:
            action()
        else:
            pl.when(condition)(action)

    def column_step(dist, sender):
        for level, exists in levels(dist):

            def act(level=level):
                if sender is other:
                    for group in range(col_ratio):
                        sibling(level, group, other).wait_recv()

                @pl.when(is_source)
                def _():
                    column_send(2 * level + sender)

            guarded(exists, act)

    def relay_step(dist):
        for level, exists in levels(dist):

            def act(level=level):
                @pl.when(relays)
                def _():
                    column_relay(2 * level)
                    column_relay(2 * level + 1)

            guarded(exists, act)

    for turn in range(col_ratio):
        high, low = col_ratio - 1 - turn, turn

        @pl.when(can_up)
        def _():
            up(0, high).start()

        @pl.when(can_down)
        def _():
            down(0, low).start()

    for group in range(col_ratio):
        sibling(z, group, core).start()
    column_step(0, core)

    for dist in range(1, depth):
        for turn in range(col_ratio):
            high, low = col_ratio - 1 - turn, turn

            @pl.when(z >= dist)
            def _():
                up_arrival(dist, high).wait_recv()

                @pl.when(can_up)
                def _():
                    up(dist, high).start()

                sibling(z - dist, high, core).start()

            @pl.when(z + dist < depth)
            def _():
                down_arrival(dist, low).wait_recv()

                @pl.when(can_down)
                def _():
                    down(dist, low).start()

                sibling(z + dist, low, core).start()

        column_step(dist, core)
        column_step(dist - 1, other)
        relay_step(dist - 1)
    column_step(depth - 1, other)
    relay_step(depth - 1)

    @pl.when(jnp.logical_not(on_source_x))
    def _():
        for piece in range(grid_cols):
            column_arrival(piece).wait_recv()

    @pl.when(is_source)
    def _():
        for piece in range(grid_cols):
            keep(piece).wait()

    for slot in range(slot_total):
        left = slot_rows_ref[0, 0, slot] // grid_rows
        right = slot_cols_ref[0, 0, slot] // grid_cols
        product = lax.dot_general(
            rows[left // col_ratio, lax.rem(left, col_ratio)],
            cols[right],
            (((1,), (1,)), ((), ())),
            preferred_element_type=jnp.float32,
        )
        live = slot < live_ref[0, 0]
        result[slot] = jnp.where(live, -product, 0.0).astype(result.dtype)
        pltpu.make_async_copy(result.at[slot], out_ref.at[0, 0, slot], store_sem.at[slot]).start()

    for dist in range(depth):
        for group in range(col_ratio):

            @pl.when(jnp.logical_and(can_up, z >= dist))
            def _():
                up(dist, group).wait_send()

            @pl.when(jnp.logical_and(can_down, z + dist < depth))
            def _():
                down(dist, group).wait_send()

    for level in range(depth):
        for group in range(col_ratio):
            sibling(level, group, core).wait_send()

    for piece in range(grid_cols):

        @pl.when(is_source)
        def _():
            for step in range(1, height):
                along_y(piece, step).wait_send()

        @pl.when(on_source_x)
        def _():
            for step in range(1, width):
                along_x(piece, step, cols.at[:, band(piece)]).wait_send()

    for slot in range(slot_total):
        pltpu.make_async_copy(result.at[slot], out_ref.at[0, 0, slot], store_sem.at[slot]).wait()


def body(grid_rows, grid_cols, panel, inverse_factor, slot_rows, slot_cols, live_count):
    panel_count, _, part_rows, tile = panel.shape
    slot_total = slot_rows.shape[-1]
    col_ratio = grid_cols // grid_rows
    column_count = panel_count // col_ratio
    depth = grid_cols // 2
    height, width = row_sides(grid_rows)
    dma = pltpu.SemaphoreType.DMA
    flops = 2 * tile * tile * (panel_count * part_rows + slot_total * tile)
    return pl.pallas_call(
        functools.partial(kernel, grid_rows, grid_cols),
        out_shape=jax.ShapeDtypeStruct((1, 1, slot_total, tile, tile), jnp.bfloat16),
        in_specs=[pl.BlockSpec(memory_space=pl.ANY)] * 2
        + [pl.BlockSpec(memory_space=pltpu.SMEM)] * 3,
        out_specs=pl.BlockSpec(memory_space=pl.ANY),
        scratch_shapes=[
            pltpu.VMEM(panel.shape, jnp.bfloat16),
            pltpu.VMEM(inverse_factor.shape, jnp.bfloat16),
            pltpu.VMEM((column_count, col_ratio, tile, tile), jnp.bfloat16),
            pltpu.VMEM((column_count, tile, tile), jnp.bfloat16),
            pltpu.VMEM((slot_total, tile, tile), jnp.bfloat16),
            dma((2,)),
            dma((slot_total,)),
            dma((grid_cols,)),
            dma((depth, col_ratio)),
            dma((depth, col_ratio)),
            dma((depth, col_ratio)),
            dma((depth, col_ratio)),
            dma((depth, col_ratio)),
            dma((depth, col_ratio)),
            dma((max(height - 1, 1), grid_cols)),
            dma((max(width - 1, 1), grid_cols)),
            dma((grid_cols,)),
        ],
        compiler_params=pltpu.CompilerParams(
            collective_id=0, has_side_effects=True, vmem_limit_bytes=32 * 1024 * 1024
        ),
        cost_estimate=pl.CostEstimate(
            flops=flops, bytes_accessed=2 * tile * tile * (1 + slot_total), transcendentals=0
        ),
    )(panel, inverse_factor, slot_rows, slot_cols, live_count)


def solution(mesh):
    placed = (
        P(None, "row", "col", None),
        P(),
        P("row", "col", None),
        P("row", "col", None),
        P("row", "col"),
    )
    return jax.shard_map(
        functools.partial(body, mesh.shape["row"], mesh.shape["col"]),
        mesh=mesh,
        in_specs=placed,
        out_specs=P("row", "col", None, None, None),
        check_vma=False,
    )
```

```python
import functools
import math

import jax
import jax.numpy as jnp
from jax import lax
from jax.experimental import pallas as pl
from jax.experimental.pallas import tpu as pltpu
from jax.sharding import PartitionSpec as P

MESH = pl.DeviceIdType.MESH


def row_sides(grid_rows):
    width = math.isqrt(grid_rows)
    while grid_rows % width:
        width -= 1
    return grid_rows // width, width


def kernel(
    grid_rows,
    grid_cols,
    panel_ref,
    inverse_ref,
    slot_rows_ref,
    slot_cols_ref,
    live_ref,
    out_ref,
    panel_buf,
    inverse_buf,
    slot_rows,
    slot_cols,
    live,
    rows,
    cols,
    result,
    load_sem,
    store_sem,
    local_sem,
    up_send,
    up_recv,
    down_send,
    down_recv,
    sib_send,
    sib_recv,
    y_send,
    x_send,
    col_recv,
):
    depth = grid_cols // 2
    height, width = row_sides(grid_rows)
    panel_count, tile, _ = rows.shape
    column_count = cols.shape[0]
    col_ratio = panel_count // column_count
    part = tile // grid_cols
    slot_total = result.shape[0]

    r = lax.axis_index("row")
    c = lax.axis_index("col")
    y, x = r // width, lax.rem(r, width)
    z, core = c // 2, lax.rem(c, 2)
    other = 1 - core
    own_group = c // grid_rows
    source = lax.rem(c, grid_rows)
    source_y, source_x = source // width, lax.rem(source, width)
    is_source = r == source
    on_source_x = x == source_x
    relays = jnp.logical_and(on_source_x, y != source_y)

    load_panel = pltpu.make_async_copy(panel_ref, panel_buf, load_sem.at[0])
    load_inverse = pltpu.make_async_copy(inverse_ref, inverse_buf, load_sem.at[1])
    load_panel.start()
    load_inverse.start()
    small = [(slot_rows_ref, slot_rows), (slot_cols_ref, slot_cols), (live_ref, live)]
    small_loads = [
        pltpu.make_async_copy(source_ref, target, load_sem.at[2 + at])
        for at, (source_ref, target) in enumerate(small)
    ]
    for load in small_loads:
        load.start()

    barrier = pltpu.get_barrier_semaphore()

    def greet(row, col):
        pl.semaphore_signal(barrier, inc=1, device_id=(row, col), device_id_type=MESH)

    greet(r, 2 * z + other)
    for step in range(1, width):
        greet(y * width + lax.rem(x + step, width), c)
    for step in range(1, height):
        greet(lax.rem(y + step, height) * width + x, c)
    can_up, can_down = z + 1 < depth, z > 0

    @pl.when(can_up)
    def _():
        greet(r, c + 2)

    @pl.when(can_down)
    def _():
        greet(r, c - 2)

    def band(piece):
        return pl.ds(pl.multiple_of(piece * part, part), part)

    load_panel.wait()
    load_inverse.wait()
    solved = jnp.dot(
        panel_buf[...].reshape(-1, tile), inverse_buf[...], preferred_element_type=jnp.float32
    )
    solved = solved.astype(jnp.bfloat16).reshape(panel_count, part, tile)
    rows[:, band(c), :] = solved

    line_peers = can_up.astype(jnp.int32) + can_down.astype(jnp.int32)
    pl.semaphore_wait(barrier, 1 + (width - 1) + (height - 1) + line_peers)

    def needed(level, a):
        return grid_rows * a + r >= 2 * level

    def guarded(condition, action):
        if condition is None:
            action()
        else:
            pl.when(condition)(action)

    def chunk_of(a, piece):
        return rows.at[a, band(piece)]

    def up(dist, a, ahead=0):
        chunk = chunk_of(a, c - 2 * dist)
        return pltpu.make_async_remote_copy(
            chunk, chunk, up_send.at[dist, a], up_recv.at[dist - ahead, a], (r, c + 2), MESH
        )

    def down(dist, a, ahead=0):
        chunk = chunk_of(a, c + 2 * dist)
        return pltpu.make_async_remote_copy(
            chunk, chunk, down_send.at[dist, a], down_recv.at[dist - ahead, a], (r, c - 2), MESH
        )

    def sibling(level, a, sender):
        chunk = chunk_of(a, 2 * level + sender)
        return pltpu.make_async_remote_copy(
            chunk,
            chunk,
            sib_send.at[level, a],
            sib_recv.at[level, a],
            (r, 2 * z + other),
            MESH,
        )

    def own_tile(k):
        return k * col_ratio + own_group

    def along_y(piece, k, step):
        return pltpu.make_async_remote_copy(
            chunk_of(own_tile(k), piece),
            cols.at[k, band(piece)],
            y_send.at[step - 1, piece, k],
            col_recv.at[piece, k],
            (lax.rem(y + step, height) * width + x, c),
            MESH,
        )

    def along_x(piece, k, step, relayed):
        return pltpu.make_async_remote_copy(
            cols.at[k, band(piece)] if relayed else chunk_of(own_tile(k), piece),
            cols.at[k, band(piece)],
            x_send.at[step - 1, piece, k],
            col_recv.at[piece, k],
            (y * width + lax.rem(x + step, width), c),
            MESH,
        )

    def keep(piece, k):
        return pltpu.make_async_copy(
            chunk_of(own_tile(k), piece), cols.at[k, band(piece)], local_sem.at[piece, k]
        )

    def column_send(piece, k, group):
        @pl.when(jnp.logical_and(is_source, own_group == group))
        def _():
            for step in range(1, height):
                along_y(piece, k, step).start()
            for step in range(1, width):
                along_x(piece, k, step, False).start()
            keep(piece, k).start()

    def column_arrival(piece, k):
        return along_x(piece, k, 1, True)

    def group_of(upward, phase):
        return col_ratio - 1 - phase if upward else phase

    def own_step(phase):
        for k in range(column_count):
            a = k * col_ratio + group_of(True, phase)
            pl.when(jnp.logical_and(can_up, needed(z + 1, a)))(lambda a=a: up(0, a).start())
            a = k * col_ratio + group_of(False, phase)
            pl.when(can_down)(lambda a=a: down(0, a).start())

    def arrive(dist, phase):
        for k in range(column_count):

            def from_below(group=group_of(True, phase), k=k):
                a = k * col_ratio + group
                up(dist, a, 1).wait_recv()
                pl.when(jnp.logical_and(can_up, needed(z + 1, a)))(lambda: up(dist, a).start())
                sibling(z - dist, a, core).start()
                column_send(c - 2 * dist, k, group)

            def from_above(group=group_of(False, phase), k=k):
                a = k * col_ratio + group
                down(dist, a, 1).wait_recv()
                pl.when(can_down)(lambda: down(dist, a).start())
                pl.when(needed(z, a))(lambda: sibling(z + dist, a, core).start())
                column_send(c + 2 * dist, k, group)

            a = k * col_ratio + group_of(True, phase)
            pl.when(jnp.logical_and(z >= dist, needed(z, a)))(from_below)
            pl.when(z + dist < depth)(from_above)

    def sibling_step(dist, phase):
        sides = [(True, z - dist, z >= dist), (False, z + dist, z + dist < depth)]
        for upward, level, exists in sides[: 1 if dist == 0 else 2]:
            for k in range(column_count):

                def act(group=group_of(upward, phase), level=level, k=k):
                    a = k * col_ratio + group

                    @pl.when(needed(z, a))
                    def _():
                        sibling(level, a, other).wait_recv()
                        column_send(2 * level + other, k, group)

                guarded(exists if dist else None, act)

    def relay_step(dist):
        sides = [(z - dist, z >= dist), (z + dist, z + dist < depth)]
        for level, exists in sides[: 1 if dist == 0 else 2]:

            def act(level=level):
                @pl.when(relays)
                def _():
                    for sender in range(2):
                        piece = 2 * level + sender
                        for k in range(column_count):
                            column_arrival(piece, k).wait_recv()
                            for step in range(1, width):
                                along_x(piece, k, step, True).start()

            guarded(exists if dist else None, act)

    phases = range(1, col_ratio)
    own_step(0)
    for a in range(panel_count):
        pl.when(needed(z, a))(lambda a=a: sibling(z, a, core).start())
    for k in range(column_count):
        for group in range(col_ratio):
            column_send(c, k, group)

    for dist in range(1, depth):
        arrive(dist, 0)
        for phase in phases:
            if dist == 1:
                own_step(phase)
            else:
                arrive(dist - 1, phase)
        sibling_step(dist - 1, 0)
        if dist == 1:
            for phase in phases:
                sibling_step(0, phase)
        else:
            for phase in phases if dist > 2 else ():
                sibling_step(dist - 2, phase)
            relay_step(dist - 2)
    sibling_step(depth - 1, 0)
    for phase in phases:
        sibling_step(depth - 2, phase)
    relay_step(depth - 2)
    relay_step(depth - 1)
    for phase in phases:
        arrive(depth - 1, phase)
    for phase in phases:
        sibling_step(depth - 1, phase)

    @pl.when(jnp.logical_not(on_source_x))
    def _():
        for piece in range(grid_cols):
            for k in range(column_count):
                column_arrival(piece, k).wait_recv()

    @pl.when(is_source)
    def _():
        for piece in range(grid_cols):
            for k in range(column_count):
                keep(piece, k).wait()

    for load in small_loads:
        load.wait()
    for slot in range(slot_total):
        left = slot_rows[0, 0, slot] // grid_rows
        right = slot_cols[0, 0, slot] // grid_cols
        product = lax.dot_general(
            rows[left],
            cols[right],
            (((1,), (1,)), ((), ())),
            preferred_element_type=jnp.float32,
        )
        alive = slot < live[0, 0]
        result[slot] = jnp.where(alive, -product, 0.0).astype(result.dtype)
        pltpu.make_async_copy(result.at[slot], out_ref.at[0, 0, slot], store_sem.at[slot]).start()

    for a in range(panel_count):
        for dist in range(depth):
            sent_up = jnp.logical_and(jnp.logical_and(can_up, z >= dist), needed(z + 1, a))
            pl.when(sent_up)(lambda a=a, dist=dist: up(dist, a).wait_send())
            sent_down = jnp.logical_and(can_down, z + dist < depth)
            pl.when(sent_down)(lambda a=a, dist=dist: down(dist, a).wait_send())

        @pl.when(needed(z, a))
        def _(a=a):
            for level in range(depth):
                sibling(level, a, core).wait_send()

    @pl.when(is_source)
    def _():
        for piece in range(grid_cols):
            for k in range(column_count):
                for step in range(1, height):
                    along_y(piece, k, step).wait_send()

    @pl.when(on_source_x)
    def _():
        for piece in range(grid_cols):
            for k in range(column_count):
                for step in range(1, width):
                    along_x(piece, k, step, True).wait_send()

    for slot in range(slot_total):
        pltpu.make_async_copy(result.at[slot], out_ref.at[0, 0, slot], store_sem.at[slot]).wait()


def body(grid_rows, grid_cols, panel, inverse_factor, slot_rows, slot_cols, live_count):
    panel_count, _, part_rows, tile = panel.shape
    slot_total = slot_rows.shape[-1]
    col_ratio = grid_cols // grid_rows
    column_count = panel_count // col_ratio
    depth = grid_cols // 2
    height, width = row_sides(grid_rows)
    dma = pltpu.SemaphoreType.DMA
    flops = 2 * tile * tile * (panel_count * part_rows + slot_total * tile)
    return pl.pallas_call(
        functools.partial(kernel, grid_rows, grid_cols),
        out_shape=jax.ShapeDtypeStruct((1, 1, slot_total, tile, tile), jnp.bfloat16),
        in_specs=[pl.BlockSpec(memory_space=pl.ANY)] * 5,
        out_specs=pl.BlockSpec(memory_space=pl.ANY),
        scratch_shapes=[
            pltpu.VMEM(panel.shape, jnp.bfloat16),
            pltpu.VMEM(inverse_factor.shape, jnp.bfloat16),
            pltpu.SMEM(slot_rows.shape, jnp.int32),
            pltpu.SMEM(slot_cols.shape, jnp.int32),
            pltpu.SMEM(live_count.shape, jnp.int32),
            pltpu.VMEM((panel_count, tile, tile), jnp.bfloat16),
            pltpu.VMEM((column_count, tile, tile), jnp.bfloat16),
            pltpu.VMEM((slot_total, tile, tile), jnp.bfloat16),
            dma((5,)),
            dma((slot_total,)),
            dma((grid_cols, column_count)),
            dma((depth, panel_count)),
            dma((depth, panel_count)),
            dma((depth, panel_count)),
            dma((depth, panel_count)),
            dma((depth, panel_count)),
            dma((depth, panel_count)),
            dma((max(height - 1, 1), grid_cols, column_count)),
            dma((max(width - 1, 1), grid_cols, column_count)),
            dma((grid_cols, column_count)),
        ],
        compiler_params=pltpu.CompilerParams(
            collective_id=0, has_side_effects=True, vmem_limit_bytes=32 * 1024 * 1024
        ),
        cost_estimate=pl.CostEstimate(
            flops=flops, bytes_accessed=2 * tile * tile * (1 + slot_total), transcendentals=0
        ),
    )(panel, inverse_factor, slot_rows, slot_cols, live_count)


def solution(mesh):
    placed = (
        P(None, "row", "col", None),
        P(),
        P("row", "col", None),
        P("row", "col", None),
        P("row", "col"),
    )
    return jax.shard_map(
        functools.partial(body, mesh.shape["row"], mesh.shape["col"]),
        mesh=mesh,
        in_specs=placed,
        out_specs=P("row", "col", None, None, None),
        check_vma=False,
    )
```

```python
import functools
import math

import jax
import jax.numpy as jnp
from jax import lax
from jax.experimental import pallas as pl
from jax.experimental.pallas import tpu as pltpu
from jax.sharding import PartitionSpec as P

MESH = pl.DeviceIdType.MESH


def row_sides(grid_rows):
    width = math.isqrt(grid_rows)
    while grid_rows % width:
        width -= 1
    return grid_rows // width, width


def kernel(
    grid_rows,
    grid_cols,
    panel_ref,
    inverse_ref,
    slot_rows_ref,
    slot_cols_ref,
    live_ref,
    out_ref,
    panel_buf,
    inverse_buf,
    slot_rows,
    slot_cols,
    live,
    rows,
    cols,
    result,
    load_sem,
    store_sem,
    local_sem,
    up_send,
    up_recv,
    down_send,
    down_recv,
    sib_send,
    sib_recv,
    y_send,
    x_send,
    col_recv,
):
    depth = grid_cols // 2
    height, width = row_sides(grid_rows)
    panel_count, tile, _ = rows.shape
    column_count = cols.shape[0]
    col_ratio = panel_count // column_count
    part = tile // grid_cols
    slot_total = result.shape[0]

    r = lax.axis_index("row")
    c = lax.axis_index("col")
    y, x = r // width, lax.rem(r, width)
    z, core = c // 2, lax.rem(c, 2)
    other = 1 - core
    own_group = c // grid_rows
    source = lax.rem(c, grid_rows)
    source_y, source_x = source // width, lax.rem(source, width)
    is_source = r == source
    on_source_x = x == source_x
    relays = jnp.logical_and(on_source_x, y != source_y)

    load_panel = pltpu.make_async_copy(panel_ref, panel_buf, load_sem.at[0])
    load_inverse = pltpu.make_async_copy(inverse_ref, inverse_buf, load_sem.at[1])
    load_panel.start()
    load_inverse.start()
    small = [(slot_rows_ref, slot_rows), (slot_cols_ref, slot_cols), (live_ref, live)]
    small_loads = [
        pltpu.make_async_copy(source_ref, target, load_sem.at[2 + at])
        for at, (source_ref, target) in enumerate(small)
    ]
    for load in small_loads:
        load.start()

    barrier = pltpu.get_barrier_semaphore()

    def greet(row, col):
        pl.semaphore_signal(barrier, inc=1, device_id=(row, col), device_id_type=MESH)

    greet(r, 2 * z + other)
    for step in range(1, width):
        greet(y * width + lax.rem(x + step, width), c)
    for step in range(1, height):
        greet(lax.rem(y + step, height) * width + x, c)
    can_up, can_down = z + 1 < depth, z > 0

    @pl.when(can_up)
    def _():
        greet(r, c + 2)

    @pl.when(can_down)
    def _():
        greet(r, c - 2)

    def band(piece):
        return pl.ds(pl.multiple_of(piece * part, part), part)

    load_panel.wait()
    load_inverse.wait()
    solved = jnp.dot(
        panel_buf[...].reshape(-1, tile), inverse_buf[...], preferred_element_type=jnp.float32
    )
    solved = solved.astype(jnp.bfloat16).reshape(panel_count, part, tile)
    rows[:, band(c), :] = solved

    line_peers = can_up.astype(jnp.int32) + can_down.astype(jnp.int32)
    pl.semaphore_wait(barrier, 1 + (width - 1) + (height - 1) + line_peers)

    def needed(level, a):
        return grid_rows * a + r >= 2 * level

    def guarded(condition, action):
        if condition is None:
            action()
        else:
            pl.when(condition)(action)

    def chunk_of(a, piece):
        return rows.at[a, band(piece)]

    def up(dist, a, ahead=0):
        chunk = chunk_of(a, c - 2 * dist)
        return pltpu.make_async_remote_copy(
            chunk, chunk, up_send.at[dist, a], up_recv.at[dist - ahead, a], (r, c + 2), MESH
        )

    def down(dist, a, ahead=0):
        chunk = chunk_of(a, c + 2 * dist)
        return pltpu.make_async_remote_copy(
            chunk, chunk, down_send.at[dist, a], down_recv.at[dist - ahead, a], (r, c - 2), MESH
        )

    def sibling(level, a, sender):
        chunk = chunk_of(a, 2 * level + sender)
        return pltpu.make_async_remote_copy(
            chunk,
            chunk,
            sib_send.at[level, a],
            sib_recv.at[level, a],
            (r, 2 * z + other),
            MESH,
        )

    def own_tile(k):
        return k * col_ratio + own_group

    def along_y(piece, k, step):
        return pltpu.make_async_remote_copy(
            chunk_of(own_tile(k), piece),
            cols.at[k, band(piece)],
            y_send.at[step - 1, piece, k],
            col_recv.at[piece, k],
            (lax.rem(y + step, height) * width + x, c),
            MESH,
        )

    def along_x(piece, k, step, relayed):
        return pltpu.make_async_remote_copy(
            cols.at[k, band(piece)] if relayed else chunk_of(own_tile(k), piece),
            cols.at[k, band(piece)],
            x_send.at[step - 1, piece, k],
            col_recv.at[piece, k],
            (y * width + lax.rem(x + step, width), c),
            MESH,
        )

    def keep(piece, k):
        return pltpu.make_async_copy(
            chunk_of(own_tile(k), piece), cols.at[k, band(piece)], local_sem.at[piece, k]
        )

    def column_send(piece, k, group):
        @pl.when(jnp.logical_and(is_source, own_group == group))
        def _():
            for step in range(1, height):
                along_y(piece, k, step).start()
            for step in range(1, width):
                along_x(piece, k, step, False).start()
            keep(piece, k).start()

    def column_arrival(piece, k):
        return along_x(piece, k, 1, True)

    def group_of(upward, phase):
        return col_ratio - 1 - phase if upward else phase

    def own_step(phase):
        for k in range(column_count):
            a = k * col_ratio + group_of(True, phase)
            pl.when(jnp.logical_and(can_up, needed(z + 1, a)))(lambda a=a: up(0, a).start())
            a = k * col_ratio + group_of(False, phase)
            pl.when(can_down)(lambda a=a: down(0, a).start())

    def arrive(dist, phase):
        for k in range(column_count):

            def from_below(group=group_of(True, phase), k=k):
                a = k * col_ratio + group
                up(dist, a, 1).wait_recv()
                pl.when(jnp.logical_and(can_up, needed(z + 1, a)))(lambda: up(dist, a).start())
                sibling(z - dist, a, core).start()
                column_send(c - 2 * dist, k, group)

            def from_above(group=group_of(False, phase), k=k):
                a = k * col_ratio + group
                down(dist, a, 1).wait_recv()
                pl.when(can_down)(lambda: down(dist, a).start())
                pl.when(needed(z, a))(lambda: sibling(z + dist, a, core).start())
                column_send(c + 2 * dist, k, group)

            a = k * col_ratio + group_of(True, phase)
            pl.when(jnp.logical_and(z >= dist, needed(z, a)))(from_below)
            pl.when(z + dist < depth)(from_above)

    def sibling_step(dist, phase):
        sides = [(True, z - dist, z >= dist), (False, z + dist, z + dist < depth)]
        for upward, level, exists in sides[: 1 if dist == 0 else 2]:
            for k in range(column_count):

                def act(group=group_of(upward, phase), level=level, k=k):
                    a = k * col_ratio + group

                    @pl.when(needed(z, a))
                    def _():
                        sibling(level, a, other).wait_recv()
                        column_send(2 * level + other, k, group)

                guarded(exists if dist else None, act)

    def relay_step(dist):
        sides = [(z - dist, z >= dist), (z + dist, z + dist < depth)]
        for level, exists in sides[: 1 if dist == 0 else 2]:

            def act(level=level):
                @pl.when(relays)
                def _():
                    for sender in range(2):
                        piece = 2 * level + sender
                        for k in range(column_count):
                            column_arrival(piece, k).wait_recv()
                            for step in range(1, width):
                                along_x(piece, k, step, True).start()

            guarded(exists if dist else None, act)

    phases = range(1, col_ratio)
    own_step(0)
    for a in range(panel_count):
        pl.when(needed(z, a))(lambda a=a: sibling(z, a, core).start())
    for k in range(column_count):
        for group in range(col_ratio):
            column_send(c, k, group)

    for dist in range(1, depth):
        arrive(dist, 0)
        for phase in phases:
            if dist == 1:
                own_step(phase)
            else:
                arrive(dist - 1, phase)
        for phase in range(col_ratio):
            sibling_step(dist - 1, phase)
        relay_step(dist - 1)
    sibling_step(depth - 1, 0)
    relay_step(depth - 1)
    for phase in phases:
        arrive(depth - 1, phase)
    for phase in phases:
        sibling_step(depth - 1, phase)

    @pl.when(jnp.logical_not(on_source_x))
    def _():
        for piece in range(grid_cols):
            for k in range(column_count):
                column_arrival(piece, k).wait_recv()

    @pl.when(is_source)
    def _():
        for piece in range(grid_cols):
            for k in range(column_count):
                keep(piece, k).wait()

    for load in small_loads:
        load.wait()
    for slot in range(slot_total):
        left = slot_rows[0, 0, slot] // grid_rows
        right = slot_cols[0, 0, slot] // grid_cols
        product = lax.dot_general(
            rows[left],
            cols[right],
            (((1,), (1,)), ((), ())),
            preferred_element_type=jnp.float32,
        )
        alive = slot < live[0, 0]
        result[slot] = jnp.where(alive, -product, 0.0).astype(result.dtype)
        pltpu.make_async_copy(result.at[slot], out_ref.at[0, 0, slot], store_sem.at[slot]).start()

    for a in range(panel_count):
        for dist in range(depth):
            sent_up = jnp.logical_and(jnp.logical_and(can_up, z >= dist), needed(z + 1, a))
            pl.when(sent_up)(lambda a=a, dist=dist: up(dist, a).wait_send())
            sent_down = jnp.logical_and(can_down, z + dist < depth)
            pl.when(sent_down)(lambda a=a, dist=dist: down(dist, a).wait_send())

        @pl.when(needed(z, a))
        def _(a=a):
            for level in range(depth):
                sibling(level, a, core).wait_send()

    @pl.when(is_source)
    def _():
        for piece in range(grid_cols):
            for k in range(column_count):
                for step in range(1, height):
                    along_y(piece, k, step).wait_send()

    @pl.when(on_source_x)
    def _():
        for piece in range(grid_cols):
            for k in range(column_count):
                for step in range(1, width):
                    along_x(piece, k, step, True).wait_send()

    for slot in range(slot_total):
        pltpu.make_async_copy(result.at[slot], out_ref.at[0, 0, slot], store_sem.at[slot]).wait()


def body(grid_rows, grid_cols, panel, inverse_factor, slot_rows, slot_cols, live_count):
    panel_count, _, part_rows, tile = panel.shape
    slot_total = slot_rows.shape[-1]
    col_ratio = grid_cols // grid_rows
    column_count = panel_count // col_ratio
    depth = grid_cols // 2
    height, width = row_sides(grid_rows)
    dma = pltpu.SemaphoreType.DMA
    flops = 2 * tile * tile * (panel_count * part_rows + slot_total * tile)
    return pl.pallas_call(
        functools.partial(kernel, grid_rows, grid_cols),
        out_shape=jax.ShapeDtypeStruct((1, 1, slot_total, tile, tile), jnp.bfloat16),
        in_specs=[pl.BlockSpec(memory_space=pltpu.HBM)] * 5,
        out_specs=pl.BlockSpec(memory_space=pl.ANY),
        scratch_shapes=[
            pltpu.VMEM(panel.shape, jnp.bfloat16),
            pltpu.VMEM(inverse_factor.shape, jnp.bfloat16),
            pltpu.SMEM(slot_rows.shape, jnp.int32),
            pltpu.SMEM(slot_cols.shape, jnp.int32),
            pltpu.SMEM(live_count.shape, jnp.int32),
            pltpu.VMEM((panel_count, tile, tile), jnp.bfloat16),
            pltpu.VMEM((column_count, tile, tile), jnp.bfloat16),
            pltpu.VMEM((slot_total, tile, tile), jnp.bfloat16),
            dma((5,)),
            dma((slot_total,)),
            dma((grid_cols, column_count)),
            dma((depth, panel_count)),
            dma((depth, panel_count)),
            dma((depth, panel_count)),
            dma((depth, panel_count)),
            dma((depth, panel_count)),
            dma((depth, panel_count)),
            dma((max(height - 1, 1), grid_cols, column_count)),
            dma((max(width - 1, 1), grid_cols, column_count)),
            dma((grid_cols, column_count)),
        ],
        compiler_params=pltpu.CompilerParams(
            collective_id=0, has_side_effects=True, vmem_limit_bytes=32 * 1024 * 1024
        ),
        cost_estimate=pl.CostEstimate(
            flops=flops, bytes_accessed=2 * tile * tile * (1 + slot_total), transcendentals=0
        ),
    )(panel, inverse_factor, slot_rows, slot_cols, live_count)


def solution(mesh):
    placed = (
        P(None, "row", "col", None),
        P(),
        P("row", "col", None),
        P("row", "col", None),
        P("row", "col"),
    )
    return jax.shard_map(
        functools.partial(body, mesh.shape["row"], mesh.shape["col"]),
        mesh=mesh,
        in_specs=placed,
        out_specs=P("row", "col", None, None, None),
        check_vma=False,
    )
```

```python
import functools
import math

import jax
import jax.numpy as jnp
from jax import lax
from jax.experimental import pallas as pl
from jax.experimental.pallas import tpu as pltpu
from jax.sharding import PartitionSpec as P

MESH = pl.DeviceIdType.MESH


def row_sides(grid_rows):
    width = math.isqrt(grid_rows)
    while grid_rows % width:
        width -= 1
    return grid_rows // width, width


def kernel(
    grid_rows,
    grid_cols,
    panel_ref,
    inverse_ref,
    slot_rows_ref,
    slot_cols_ref,
    live_ref,
    out_ref,
    panel_buf,
    inverse_buf,
    slot_rows,
    slot_cols,
    live,
    rows,
    cols,
    result,
    load_sem,
    store_sem,
    local_sem,
    up_send,
    up_recv,
    down_send,
    down_recv,
    sib_send,
    sib_recv,
    y_send,
    x_send,
    col_recv,
):
    depth = grid_cols // 2
    height, width = row_sides(grid_rows)
    panel_count, tile, _ = rows.shape
    column_count = cols.shape[0]
    col_ratio = panel_count // column_count
    part = tile // grid_cols
    slot_total = result.shape[0]

    r = lax.axis_index("row")
    c = lax.axis_index("col")
    y, x = r // width, lax.rem(r, width)
    z, core = c // 2, lax.rem(c, 2)
    other = 1 - core
    own_group = c // grid_rows
    source = lax.rem(c, grid_rows)
    source_y, source_x = source // width, lax.rem(source, width)
    is_source = r == source
    on_source_x = x == source_x
    relays = jnp.logical_and(on_source_x, y != source_y)

    load_panel = pltpu.make_async_copy(panel_ref, panel_buf, load_sem.at[0])
    load_inverse = pltpu.make_async_copy(inverse_ref, inverse_buf, load_sem.at[1])
    load_panel.start()
    load_inverse.start()
    small = [(slot_rows_ref, slot_rows), (slot_cols_ref, slot_cols), (live_ref, live)]
    small_loads = [
        pltpu.make_async_copy(source_ref, target, load_sem.at[2 + at])
        for at, (source_ref, target) in enumerate(small)
    ]
    for load in small_loads:
        load.start()

    barrier = pltpu.get_barrier_semaphore()

    def greet(row, col):
        pl.semaphore_signal(barrier, inc=1, device_id=(row, col), device_id_type=MESH)

    greet(r, 2 * z + other)
    for step in range(1, width):
        greet(y * width + lax.rem(x + step, width), c)
    for step in range(1, height):
        greet(lax.rem(y + step, height) * width + x, c)
    can_up, can_down = z + 1 < depth, z > 0

    @pl.when(can_up)
    def _():
        greet(r, c + 2)

    @pl.when(can_down)
    def _():
        greet(r, c - 2)

    def band(piece):
        return pl.ds(pl.multiple_of(piece * part, part), part)

    load_panel.wait()
    load_inverse.wait()
    solved = jnp.dot(
        panel_buf[...].reshape(-1, tile), inverse_buf[...], preferred_element_type=jnp.float32
    )
    solved = solved.astype(jnp.bfloat16).reshape(panel_count, part, tile)
    rows[:, band(c), :] = solved

    line_peers = can_up.astype(jnp.int32) + can_down.astype(jnp.int32)
    pl.semaphore_wait(barrier, 1 + (width - 1) + (height - 1) + line_peers)

    def needed(level, a):
        return grid_rows * a + r >= 2 * level

    def guarded(condition, action):
        if condition is None:
            action()
        else:
            pl.when(condition)(action)

    def chunk_of(a, piece):
        return rows.at[a, band(piece)]

    def up(dist, a, ahead=0):
        chunk = chunk_of(a, c - 2 * dist)
        return pltpu.make_async_remote_copy(
            chunk, chunk, up_send.at[dist, a], up_recv.at[dist - ahead, a], (r, c + 2), MESH
        )

    def down(dist, a, ahead=0):
        chunk = chunk_of(a, c + 2 * dist)
        return pltpu.make_async_remote_copy(
            chunk, chunk, down_send.at[dist, a], down_recv.at[dist - ahead, a], (r, c - 2), MESH
        )

    def sibling(level, a, sender):
        chunk = chunk_of(a, 2 * level + sender)
        return pltpu.make_async_remote_copy(
            chunk,
            chunk,
            sib_send.at[level, a],
            sib_recv.at[level, a],
            (r, 2 * z + other),
            MESH,
        )

    def own_tile(k):
        return k * col_ratio + own_group

    def along_y(piece, k, step):
        return pltpu.make_async_remote_copy(
            chunk_of(own_tile(k), piece),
            cols.at[k, band(piece)],
            y_send.at[step - 1, piece, k],
            col_recv.at[piece, k],
            (lax.rem(y + step, height) * width + x, c),
            MESH,
        )

    def along_x(piece, k, step, relayed):
        return pltpu.make_async_remote_copy(
            cols.at[k, band(piece)] if relayed else chunk_of(own_tile(k), piece),
            cols.at[k, band(piece)],
            x_send.at[step - 1, piece, k],
            col_recv.at[piece, k],
            (y * width + lax.rem(x + step, width), c),
            MESH,
        )

    def keep(piece, k):
        return pltpu.make_async_copy(
            chunk_of(own_tile(k), piece), cols.at[k, band(piece)], local_sem.at[piece, k]
        )

    def column_send(piece, k, group):
        @pl.when(jnp.logical_and(is_source, own_group == group))
        def _():
            for step in range(1, height):
                along_y(piece, k, step).start()
            for step in range(1, width):
                along_x(piece, k, step, False).start()
            keep(piece, k).start()

    def column_arrival(piece, k):
        return along_x(piece, k, 1, True)

    def group_of(upward, phase):
        return col_ratio - 1 - phase if upward else phase

    def own_step(phase):
        for k in range(column_count):
            a = k * col_ratio + group_of(True, phase)
            pl.when(jnp.logical_and(can_up, needed(z + 1, a)))(lambda a=a: up(0, a).start())
            a = k * col_ratio + group_of(False, phase)
            pl.when(can_down)(lambda a=a: down(0, a).start())

    def arrive(dist, phase):
        for k in range(column_count):

            def from_below(group=group_of(True, phase), k=k):
                a = k * col_ratio + group
                up(dist, a, 1).wait_recv()
                pl.when(jnp.logical_and(can_up, needed(z + 1, a)))(lambda: up(dist, a).start())
                sibling(z - dist, a, core).start()
                column_send(c - 2 * dist, k, group)

            def from_above(group=group_of(False, phase), k=k):
                a = k * col_ratio + group
                down(dist, a, 1).wait_recv()
                pl.when(can_down)(lambda: down(dist, a).start())
                pl.when(needed(z, a))(lambda: sibling(z + dist, a, core).start())
                column_send(c + 2 * dist, k, group)

            a = k * col_ratio + group_of(True, phase)
            pl.when(jnp.logical_and(z >= dist, needed(z, a)))(from_below)
            pl.when(z + dist < depth)(from_above)

    def sibling_step(dist, phase):
        sides = [(True, z - dist, z >= dist), (False, z + dist, z + dist < depth)]
        for upward, level, exists in sides[: 1 if dist == 0 else 2]:
            for k in range(column_count):

                def act(group=group_of(upward, phase), level=level, k=k):
                    a = k * col_ratio + group

                    @pl.when(needed(z, a))
                    def _():
                        sibling(level, a, other).wait_recv()
                        column_send(2 * level + other, k, group)

                guarded(exists if dist else None, act)

    def relay_step(dist, phase):
        sides = [(True, z - dist, z >= dist), (False, z + dist, z + dist < depth)]
        for upward, level, exists in sides[: 1 if dist == 0 else 2]:
            mine = relays
            if dist:
                mine = jnp.logical_and(relays, own_group == group_of(upward, phase))
                mine = jnp.logical_and(mine, exists)

            @pl.when(mine)
            def _(level=level):
                for sender in range(2):
                    piece = 2 * level + sender
                    for k in range(column_count):
                        column_arrival(piece, k).wait_recv()
                        for step in range(1, width):
                            along_x(piece, k, step, True).start()

    phases = range(1, col_ratio)
    own_step(0)
    for a in range(panel_count):
        pl.when(needed(z, a))(lambda a=a: sibling(z, a, core).start())
    for k in range(column_count):
        for group in range(col_ratio):
            column_send(c, k, group)

    for dist in range(1, depth):
        arrive(dist, 0)
        if dist == 1:
            for phase in phases:
                own_step(phase)
            for phase in range(col_ratio):
                sibling_step(0, phase)
        sibling_step(dist, 0)
        if dist == 1:
            relay_step(0, 0)
            continue
        if dist == 2:
            relay_step(1, 0)
        for phase in phases:
            arrive(dist - 1, phase)
        for phase in phases:
            sibling_step(dist - 1, phase)
        relay_step(dist, 0)
        for phase in phases:
            relay_step(dist - 1, phase)
    for phase in phases:
        arrive(depth - 1, phase)
    for phase in phases:
        sibling_step(depth - 1, phase)
    for phase in phases:
        relay_step(depth - 1, phase)

    @pl.when(jnp.logical_not(on_source_x))
    def _():
        for piece in range(grid_cols):
            for k in range(column_count):
                column_arrival(piece, k).wait_recv()

    @pl.when(is_source)
    def _():
        for piece in range(grid_cols):
            for k in range(column_count):
                keep(piece, k).wait()

    for load in small_loads:
        load.wait()
    for slot in range(slot_total):
        left = slot_rows[0, 0, slot] // grid_rows
        right = slot_cols[0, 0, slot] // grid_cols
        product = lax.dot_general(
            rows[left],
            cols[right],
            (((1,), (1,)), ((), ())),
            preferred_element_type=jnp.float32,
        )
        alive = slot < live[0, 0]
        result[slot] = jnp.where(alive, -product, 0.0).astype(result.dtype)
        pltpu.make_async_copy(result.at[slot], out_ref.at[0, 0, slot], store_sem.at[slot]).start()

    for a in range(panel_count):
        for dist in range(depth):
            sent_up = jnp.logical_and(jnp.logical_and(can_up, z >= dist), needed(z + 1, a))
            pl.when(sent_up)(lambda a=a, dist=dist: up(dist, a).wait_send())
            sent_down = jnp.logical_and(can_down, z + dist < depth)
            pl.when(sent_down)(lambda a=a, dist=dist: down(dist, a).wait_send())

        @pl.when(needed(z, a))
        def _(a=a):
            for level in range(depth):
                sibling(level, a, core).wait_send()

    @pl.when(is_source)
    def _():
        for piece in range(grid_cols):
            for k in range(column_count):
                for step in range(1, height):
                    along_y(piece, k, step).wait_send()

    @pl.when(on_source_x)
    def _():
        for piece in range(grid_cols):
            for k in range(column_count):
                for step in range(1, width):
                    along_x(piece, k, step, True).wait_send()

    for slot in range(slot_total):
        pltpu.make_async_copy(result.at[slot], out_ref.at[0, 0, slot], store_sem.at[slot]).wait()


def body(grid_rows, grid_cols, panel, inverse_factor, slot_rows, slot_cols, live_count):
    panel_count, _, part_rows, tile = panel.shape
    slot_total = slot_rows.shape[-1]
    col_ratio = grid_cols // grid_rows
    column_count = panel_count // col_ratio
    depth = grid_cols // 2
    height, width = row_sides(grid_rows)
    dma = pltpu.SemaphoreType.DMA
    flops = 2 * tile * tile * (panel_count * part_rows + slot_total * tile)
    return pl.pallas_call(
        functools.partial(kernel, grid_rows, grid_cols),
        out_shape=jax.ShapeDtypeStruct((1, 1, slot_total, tile, tile), jnp.bfloat16),
        in_specs=[pl.BlockSpec(memory_space=pl.ANY)] * 5,
        out_specs=pl.BlockSpec(memory_space=pl.ANY),
        scratch_shapes=[
            pltpu.VMEM(panel.shape, jnp.bfloat16),
            pltpu.VMEM(inverse_factor.shape, jnp.bfloat16),
            pltpu.SMEM(slot_rows.shape, jnp.int32),
            pltpu.SMEM(slot_cols.shape, jnp.int32),
            pltpu.SMEM(live_count.shape, jnp.int32),
            pltpu.VMEM((panel_count, tile, tile), jnp.bfloat16),
            pltpu.VMEM((column_count, tile, tile), jnp.bfloat16),
            pltpu.VMEM((slot_total, tile, tile), jnp.bfloat16),
            dma((5,)),
            dma((slot_total,)),
            dma((grid_cols, column_count)),
            dma((depth, panel_count)),
            dma((depth, panel_count)),
            dma((depth, panel_count)),
            dma((depth, panel_count)),
            dma((depth, panel_count)),
            dma((depth, panel_count)),
            dma((max(height - 1, 1), grid_cols, column_count)),
            dma((max(width - 1, 1), grid_cols, column_count)),
            dma((grid_cols, column_count)),
        ],
        compiler_params=pltpu.CompilerParams(
            collective_id=0, has_side_effects=True, vmem_limit_bytes=60 * 1024 * 1024
        ),
        cost_estimate=pl.CostEstimate(
            flops=flops, bytes_accessed=2 * tile * tile * (1 + slot_total), transcendentals=0
        ),
    )(panel, inverse_factor, slot_rows, slot_cols, live_count)


def solution(mesh):
    placed = (
        P(None, "row", "col", None),
        P(),
        P("row", "col", None),
        P("row", "col", None),
        P("row", "col"),
    )
    return jax.shard_map(
        functools.partial(body, mesh.shape["row"], mesh.shape["col"]),
        mesh=mesh,
        in_specs=placed,
        out_specs=P("row", "col", None, None, None),
        check_vma=False,
    )
```

```python
import functools
import math

import jax
import jax.numpy as jnp
from jax import lax
from jax.experimental import pallas as pl
from jax.experimental.pallas import tpu as pltpu
from jax.sharding import PartitionSpec as P

MESH = pl.DeviceIdType.MESH


def row_sides(grid_rows):
    width = math.isqrt(grid_rows)
    while grid_rows % width:
        width -= 1
    return grid_rows // width, width


def kernel(
    grid_rows,
    grid_cols,
    panel_ref,
    inverse_ref,
    slot_rows_ref,
    slot_cols_ref,
    live_ref,
    out_ref,
    panel_buf,
    inverse_buf,
    slot_rows,
    slot_cols,
    live,
    rows,
    cols,
    result,
    load_sem,
    store_sem,
    local_sem,
    up_send,
    up_recv,
    down_send,
    down_recv,
    sib_send,
    sib_recv,
    y_send,
    x_send,
    col_recv,
):
    depth = grid_cols // 2
    height, width = row_sides(grid_rows)
    panel_count, tile, _ = rows.shape
    column_count = cols.shape[0]
    col_ratio = panel_count // column_count
    part = tile // grid_cols
    slot_total = result.shape[0]

    r = lax.axis_index("row")
    c = lax.axis_index("col")
    y, x = r // width, lax.rem(r, width)
    z, core = c // 2, lax.rem(c, 2)
    other = 1 - core
    own_group = c // grid_rows
    source = lax.rem(c, grid_rows)
    source_y, source_x = source // width, lax.rem(source, width)
    is_source = r == source
    on_source_x = x == source_x
    relays = jnp.logical_and(on_source_x, y != source_y)

    load_panel = pltpu.make_async_copy(panel_ref, panel_buf, load_sem.at[0])
    load_inverse = pltpu.make_async_copy(inverse_ref, inverse_buf, load_sem.at[1])
    load_panel.start()
    load_inverse.start()
    small = [(slot_rows_ref, slot_rows), (slot_cols_ref, slot_cols), (live_ref, live)]
    small_loads = [
        pltpu.make_async_copy(source_ref, target, load_sem.at[2 + at])
        for at, (source_ref, target) in enumerate(small)
    ]
    for load in small_loads:
        load.start()

    barrier = pltpu.get_barrier_semaphore()

    def greet(row, col):
        pl.semaphore_signal(barrier, inc=1, device_id=(row, col), device_id_type=MESH)

    greet(r, 2 * z + other)
    for step in range(1, width):
        greet(y * width + lax.rem(x + step, width), c)
    for step in range(1, height):
        greet(lax.rem(y + step, height) * width + x, c)
    can_up, can_down = z + 1 < depth, z > 0

    @pl.when(can_up)
    def _():
        greet(r, c + 2)

    @pl.when(can_down)
    def _():
        greet(r, c - 2)

    def band(piece):
        return pl.ds(pl.multiple_of(piece * part, part), part)

    load_panel.wait()
    load_inverse.wait()
    solved = jnp.dot(
        panel_buf[...].reshape(-1, tile), inverse_buf[...], preferred_element_type=jnp.float32
    )
    solved = solved.astype(jnp.bfloat16).reshape(panel_count, part, tile)
    rows[:, band(c), :] = solved

    line_peers = can_up.astype(jnp.int32) + can_down.astype(jnp.int32)
    pl.semaphore_wait(barrier, 1 + (width - 1) + (height - 1) + line_peers)

    def needed(level, a):
        return grid_rows * a + r >= 2 * level

    def guarded(condition, action):
        if condition is None:
            action()
        else:
            pl.when(condition)(action)

    def chunk_of(a, piece):
        return rows.at[a, band(piece)]

    def up(dist, a, ahead=0):
        chunk = chunk_of(a, c - 2 * dist)
        return pltpu.make_async_remote_copy(
            chunk, chunk, up_send.at[dist, a], up_recv.at[dist - ahead, a], (r, c + 2), MESH
        )

    def down(dist, a, ahead=0):
        chunk = chunk_of(a, c + 2 * dist)
        return pltpu.make_async_remote_copy(
            chunk, chunk, down_send.at[dist, a], down_recv.at[dist - ahead, a], (r, c - 2), MESH
        )

    def sibling(level, a, sender):
        chunk = chunk_of(a, 2 * level + sender)
        return pltpu.make_async_remote_copy(
            chunk,
            chunk,
            sib_send.at[level, a],
            sib_recv.at[level, a],
            (r, 2 * z + other),
            MESH,
        )

    def own_tile(k):
        return k * col_ratio + own_group

    def along_y(piece, k, step):
        return pltpu.make_async_remote_copy(
            chunk_of(own_tile(k), piece),
            cols.at[k, band(piece)],
            y_send.at[step - 1, piece, k],
            col_recv.at[piece, k],
            (lax.rem(y + step, height) * width + x, c),
            MESH,
        )

    def along_x(piece, k, step, relayed):
        return pltpu.make_async_remote_copy(
            cols.at[k, band(piece)] if relayed else chunk_of(own_tile(k), piece),
            cols.at[k, band(piece)],
            x_send.at[step - 1, piece, k],
            col_recv.at[piece, k],
            (y * width + lax.rem(x + step, width), c),
            MESH,
        )

    def keep(piece, k):
        return pltpu.make_async_copy(
            chunk_of(own_tile(k), piece), cols.at[k, band(piece)], local_sem.at[piece, k]
        )

    def column_send(piece, k, group):
        @pl.when(jnp.logical_and(is_source, own_group == group))
        def _():
            for step in range(1, height):
                along_y(piece, k, step).start()
            for step in range(1, width):
                along_x(piece, k, step, False).start()
            keep(piece, k).start()

    def column_arrival(piece, k):
        return along_x(piece, k, 1, True)

    def group_of(upward, phase):
        return col_ratio - 1 - phase if upward else phase

    def own_step(phase):
        for k in range(column_count):
            a = k * col_ratio + group_of(True, phase)
            pl.when(jnp.logical_and(can_up, needed(z + 1, a)))(lambda a=a: up(0, a).start())
            a = k * col_ratio + group_of(False, phase)
            pl.when(can_down)(lambda a=a: down(0, a).start())

    def arrive(dist, phase):
        for k in range(column_count):

            def from_below(group=group_of(True, phase), k=k):
                a = k * col_ratio + group
                up(dist, a, 1).wait_recv()
                pl.when(jnp.logical_and(can_up, needed(z + 1, a)))(lambda: up(dist, a).start())
                sibling(z - dist, a, core).start()
                column_send(c - 2 * dist, k, group)

            def from_above(group=group_of(False, phase), k=k):
                a = k * col_ratio + group
                down(dist, a, 1).wait_recv()
                pl.when(can_down)(lambda: down(dist, a).start())
                pl.when(needed(z, a))(lambda: sibling(z + dist, a, core).start())
                column_send(c + 2 * dist, k, group)

            a = k * col_ratio + group_of(True, phase)
            pl.when(jnp.logical_and(z >= dist, needed(z, a)))(from_below)
            pl.when(z + dist < depth)(from_above)

    def sibling_step(dist, phase):
        sides = [(True, z - dist, z >= dist), (False, z + dist, z + dist < depth)]
        for upward, level, exists in sides[: 1 if dist == 0 else 2]:
            for k in range(column_count):

                def act(group=group_of(upward, phase), level=level, k=k):
                    a = k * col_ratio + group

                    @pl.when(needed(z, a))
                    def _():
                        sibling(level, a, other).wait_recv()
                        column_send(2 * level + other, k, group)

                guarded(exists if dist else None, act)

    def relay_step(dist, phase, place):
        sides = [(True, z - dist, z >= dist), (False, z + dist, z + dist < depth)]
        for upward, level, exists in sides[: 1 if dist == 0 else 2]:
            mine = jnp.logical_and(relays, place)
            if dist:
                mine = jnp.logical_and(mine, own_group == group_of(upward, phase))
                mine = jnp.logical_and(mine, exists)

            @pl.when(mine)
            def _(level=level):
                for sender in range(2):
                    piece = 2 * level + sender
                    for k in range(column_count):
                        column_arrival(piece, k).wait_recv()
                        for step in range(1, width):
                            along_x(piece, k, step, True).start()

    phases = range(1, col_ratio)
    between = jnp.logical_and(can_up, can_down)
    at_end = jnp.logical_not(between)
    own_step(0)
    for a in range(panel_count):
        pl.when(needed(z, a))(lambda a=a: sibling(z, a, core).start())
    for k in range(column_count):
        for group in range(col_ratio):
            column_send(c, k, group)

    for dist in range(1, depth):
        arrive(dist, 0)
        if dist == 1:
            for phase in phases:
                own_step(phase)
            for phase in range(col_ratio):
                sibling_step(0, phase)
        sibling_step(dist, 0)
        if dist == 1:
            relay_step(0, 0, z >= 0)
            continue
        if dist == 2:
            relay_step(1, 0, at_end)
        for phase in phases:
            arrive(dist - 1, phase)
        for phase in phases:
            sibling_step(dist - 1, phase)
        relay_step(dist - 1, 0, between)
        if dist > 2:
            for phase in phases:
                relay_step(dist - 2, phase, between)
        relay_step(dist, 0, at_end)
        for phase in phases:
            relay_step(dist - 1, phase, at_end)
    for phase in phases:
        arrive(depth - 1, phase)
    for phase in phases:
        sibling_step(depth - 1, phase)
    relay_step(depth - 1, 0, between)
    for phase in phases:
        relay_step(depth - 2, phase, between)
        relay_step(depth - 1, phase, z >= 0)

    @pl.when(jnp.logical_not(on_source_x))
    def _():
        for piece in range(grid_cols):
            for k in range(column_count):
                column_arrival(piece, k).wait_recv()

    @pl.when(is_source)
    def _():
        for piece in range(grid_cols):
            for k in range(column_count):
                keep(piece, k).wait()

    for load in small_loads:
        load.wait()
    for slot in range(slot_total):
        left = slot_rows[0, 0, slot] // grid_rows
        right = slot_cols[0, 0, slot] // grid_cols
        product = lax.dot_general(
            rows[left],
            cols[right],
            (((1,), (1,)), ((), ())),
            preferred_element_type=jnp.float32,
        )
        alive = slot < live[0, 0]
        result[slot] = jnp.where(alive, -product, 0.0).astype(result.dtype)
        pltpu.make_async_copy(result.at[slot], out_ref.at[0, 0, slot], store_sem.at[slot]).start()

    for a in range(panel_count):
        for dist in range(depth):
            sent_up = jnp.logical_and(jnp.logical_and(can_up, z >= dist), needed(z + 1, a))
            pl.when(sent_up)(lambda a=a, dist=dist: up(dist, a).wait_send())
            sent_down = jnp.logical_and(can_down, z + dist < depth)
            pl.when(sent_down)(lambda a=a, dist=dist: down(dist, a).wait_send())

        @pl.when(needed(z, a))
        def _(a=a):
            for level in range(depth):
                sibling(level, a, core).wait_send()

    @pl.when(is_source)
    def _():
        for piece in range(grid_cols):
            for k in range(column_count):
                for step in range(1, height):
                    along_y(piece, k, step).wait_send()

    @pl.when(on_source_x)
    def _():
        for piece in range(grid_cols):
            for k in range(column_count):
                for step in range(1, width):
                    along_x(piece, k, step, True).wait_send()

    for slot in range(slot_total):
        pltpu.make_async_copy(result.at[slot], out_ref.at[0, 0, slot], store_sem.at[slot]).wait()


def body(grid_rows, grid_cols, panel, inverse_factor, slot_rows, slot_cols, live_count):
    panel_count, _, part_rows, tile = panel.shape
    slot_total = slot_rows.shape[-1]
    col_ratio = grid_cols // grid_rows
    column_count = panel_count // col_ratio
    depth = grid_cols // 2
    height, width = row_sides(grid_rows)
    dma = pltpu.SemaphoreType.DMA
    flops = 2 * tile * tile * (panel_count * part_rows + slot_total * tile)
    return pl.pallas_call(
        functools.partial(kernel, grid_rows, grid_cols),
        out_shape=jax.ShapeDtypeStruct((1, 1, slot_total, tile, tile), jnp.bfloat16),
        in_specs=[pl.BlockSpec(memory_space=pl.ANY)] * 5,
        out_specs=pl.BlockSpec(memory_space=pl.ANY),
        scratch_shapes=[
            pltpu.VMEM(panel.shape, jnp.bfloat16),
            pltpu.VMEM(inverse_factor.shape, jnp.bfloat16),
            pltpu.SMEM(slot_rows.shape, jnp.int32),
            pltpu.SMEM(slot_cols.shape, jnp.int32),
            pltpu.SMEM(live_count.shape, jnp.int32),
            pltpu.VMEM((panel_count, tile, tile), jnp.bfloat16),
            pltpu.VMEM((column_count, tile, tile), jnp.bfloat16),
            pltpu.VMEM((slot_total, tile, tile), jnp.bfloat16),
            dma((5,)),
            dma((slot_total,)),
            dma((grid_cols, column_count)),
            dma((depth, panel_count)),
            dma((depth, panel_count)),
            dma((depth, panel_count)),
            dma((depth, panel_count)),
            dma((depth, panel_count)),
            dma((depth, panel_count)),
            dma((max(height - 1, 1), grid_cols, column_count)),
            dma((max(width - 1, 1), grid_cols, column_count)),
            dma((grid_cols, column_count)),
        ],
        compiler_params=pltpu.CompilerParams(
            collective_id=0, has_side_effects=True, vmem_limit_bytes=60 * 1024 * 1024
        ),
        cost_estimate=pl.CostEstimate(
            flops=flops, bytes_accessed=2 * tile * tile * (1 + slot_total), transcendentals=0
        ),
    )(panel, inverse_factor, slot_rows, slot_cols, live_count)


def solution(mesh):
    placed = (
        P(None, "row", "col", None),
        P(),
        P("row", "col", None),
        P("row", "col", None),
        P("row", "col"),
    )
    return jax.shard_map(
        functools.partial(body, mesh.shape["row"], mesh.shape["col"]),
        mesh=mesh,
        in_specs=placed,
        out_specs=P("row", "col", None, None, None),
        check_vma=False,
    )
```
